128 devices in a mesh: dp: 8 (over y, x_lo), ctx: 16 (over x_hi, z, core).
Axes of the slice: x: 4 (x_hi: 2, x_lo: 2; x = x_hi * 2 + x_lo), y: 4, z: 4, core: 2. Of those that a mesh axis runs over, the one named last changes fastest.
Arguments:
- queries: bfloat16 [32768, 1024], P(('dp', 'ctx')), parts along dimension 0, may hold values from -6 to 6
- keys: bfloat16 [32768, 1024], P(('dp', 'ctx')), parts along dimension 0, may hold values from -6 to 6
- values: bfloat16 [32768, 1024], P(('dp', 'ctx')), parts along dimension 0, may hold values from -6 to 6
- grad_out: bfloat16 [32768, 1024], P(('dp', 'ctx')), parts along dimension 0, may hold values from -6 to 6
Outputs:
- attended: bfloat16 [32768, 1024], P(('dp', 'ctx')), parts along dimension 0
- query_grads: bfloat16 [32768, 1024], P(('dp', 'ctx')), parts along dimension 0
- key_grads: bfloat16 [32768, 1024], P(('dp', 'ctx')), parts along dimension 0
- value_grads: bfloat16 [32768, 1024], P(('dp', 'ctx')), parts along dimension 0
The draws below stay inside these ranges and needn't reach their ends.
There are 8 independent parts, one for each index of `dp`. The reference program is written for one: setup_inputs(seed, part) draws one part's arguments, and reference() takes and returns one part's arrays. A program takes and returns all parts, laid end to end along the dimension named above; each array names one. Nothing has to cross between parts.
All inputs are finite; a program needn't handle non-finite values.
Results may differ from the reference program's by a relative error of at most 0.025.
Values may be sent and summed in bfloat16 or wider, within the bound.
No kernel may reach another device: no remote copies, remote signals or barrier semaphores. Data moves between devices by JAX's collectives and lax.ppermute only.
A program may use at most 192 MiB of HBM per device.

```python
import jax
import jax.numpy as jnp
from jax import lax

HEAD = 128
HEADS = 8
TOKENS = 4096


def draw_queries(key, part):
    key = jax.random.fold_in(key, 11)
    field = jnp.clip(1.5 * jax.random.normal(key, (TOKENS, HEADS * HEAD), jnp.float32), -6.0, 6.0)
    return field.astype(jnp.bfloat16)


def draw_keys(key, part):
    key = jax.random.fold_in(key, 23)
    field = jnp.clip(1.5 * jax.random.normal(key, (TOKENS, HEADS * HEAD), jnp.float32), -6.0, 6.0)
    return field.astype(jnp.bfloat16)


def levels(rng, shape, cuts, smallest, largest):
    factor_of = 1.0
    for axis_at, shards_of in cuts:
        heights = jax.random.uniform(jax.random.fold_in(jax.random.fold_in(rng, 6), axis_at), (shards_of,), jnp.float32, smallest / len(cuts), largest / len(cuts))
        factor_of = factor_of * jnp.repeat(jnp.exp(heights), shape[axis_at] // shards_of).reshape((-1,) + (1,) * (len(shape) - 1 - axis_at))
    return factor_of


def noise(own_key, dims, deviation, limit, pieces=(), held_as=jnp.bfloat16):
    values = deviation * jax.random.normal(own_key, dims, jnp.float32)
    if pieces:
        values = values * levels(own_key, dims, pieces, -0.22, 0.18)
    return jnp.clip(values, -limit, limit).astype(held_as)


def setup_inputs(seed: int = 0, part: int = 0) -> dict:
    streams_of = jax.random.split(jax.random.key(seed), 5)
    own_keys = jax.random.split(jax.random.fold_in(streams_of[4], part), 5)
    queries = draw_queries(jax.random.fold_in(jax.random.fold_in(streams_of[4], part), 71), part)
    keys = draw_keys(jax.random.fold_in(jax.random.fold_in(streams_of[4], part), 71), part)
    values = noise(own_keys[2], (TOKENS, HEADS * HEAD), 1.0, 6.0, ((0, 16),))
    grad_out = noise(own_keys[3], (TOKENS, HEADS * HEAD), 1.0, 6.0, ((0, 16),))
    return {"queries": queries, "keys": keys, "values": values, "grad_out": grad_out}


def head_pass(inputs):
    query_head, key_head, value_head, cotangent = inputs
    softmax_scale = HEAD ** -0.5
    scores = jnp.dot(query_head, key_head.T, preferred_element_type=jnp.float32) * softmax_scale
    row_max = jnp.max(scores, axis=1, keepdims=True)
    log_total = row_max + jnp.log(jnp.sum(jnp.exp(scores - row_max), axis=1, keepdims=True))
    weights = jnp.exp(scores - log_total).astype(jnp.bfloat16)
    attended = jnp.dot(weights, value_head, preferred_element_type=jnp.float32).astype(jnp.bfloat16)
    row_dots = jnp.sum(cotangent.astype(jnp.float32) * attended.astype(jnp.float32), axis=1, keepdims=True)
    weight_grads = jnp.dot(cotangent, value_head.T, preferred_element_type=jnp.float32)
    score_grads = (weights.astype(jnp.float32) * (weight_grads - row_dots)).astype(jnp.bfloat16)
    value_grads = jnp.dot(weights.T, cotangent, preferred_element_type=jnp.float32).astype(jnp.bfloat16)
    query_grads = (softmax_scale * jnp.dot(score_grads, key_head, preferred_element_type=jnp.float32)).astype(jnp.bfloat16)
    key_grads = (softmax_scale * jnp.dot(score_grads.T, query_head, preferred_element_type=jnp.float32)).astype(jnp.bfloat16)
    return attended, query_grads, key_grads, value_grads


def split_heads(array):
    return jnp.transpose(array.reshape(TOKENS, HEADS, HEAD), (1, 0, 2))


def join_heads(array):
    return jnp.transpose(array, (1, 0, 2)).reshape(TOKENS, HEADS * HEAD)


def reference(queries, keys, values, grad_out):
    results = lax.map(head_pass, (split_heads(queries), split_heads(keys), split_heads(values), split_heads(grad_out)))
    return (join_heads(results[0]), join_heads(results[1]), join_heads(results[2]), join_heads(results[3]))
```

```python
import functools

import jax
import jax.numpy as jnp
from jax import lax
from jax.experimental import pallas as pl
from jax.experimental.pallas import tpu as pltpu
from jax.sharding import PartitionSpec as P

HEAD = 128
HEADS = 8
SCALE = HEAD**-0.5
LOG2E = 1.4426950408889634
F32 = jnp.float32
BF16 = jnp.bfloat16
NN = (((1,), (0,)), ((), ()))
NT = (((1,), (1,)), ((), ()))
VMEM_LIMIT = 60 * 2**20


def dot(a, b, dims):
    return lax.dot_general(a, b, dims, preferred_element_type=F32)


def rows(i, size):
    return pl.ds(pl.multiple_of(i * size, size), size)


def attention_kernel(
    key_block,
    qd_ref,
    kv_ref,
    kv_far_ref,
    oq_ref,
    near_ref,
    far_ref,
    kk_ref,
    va_ref,
    kt_ref,
    vt_ref,
    q2_ref,
    da_ref,
    s_ref,
    e_ref,
    dk_ref,
    dv_ref,
):
    queries = qd_ref.shape[0]
    half = kv_ref.shape[0]
    keys = 2 * half
    query_block = s_ref.shape[1]
    chunks = keys // key_block
    half_chunks = half // key_block

    def prepare(source, base):
        def step(i, _):
            k = source[rows(i, key_block), 0:HEAD]
            v = source[rows(i, key_block), HEAD : 2 * HEAD]
            to = rows(i + base, key_block)
            kk_ref[to, 0:HEAD] = k
            kk_ref[to, HEAD : 2 * HEAD] = k
            va_ref[to, 0:HEAD] = v
            lane = lax.broadcasted_iota(jnp.int32, (key_block, HEAD), 1)
            va_ref[to, HEAD : 2 * HEAD] = jnp.where(lane < 2, 1.0, 0.0).astype(BF16)
            kt_ref[:, to] = k.T
            vt_ref[0:HEAD, to] = v.T
            vt_ref[HEAD : HEAD + 16, to] = jnp.ones((16, key_block), BF16)
            return 0

        lax.fori_loop(0, half_chunks, step, 0)

    prepare(kv_ref, 0)
    prepare(kv_far_ref, half_chunks)

    def block(b, _):
        at = rows(b, query_block)
        q = qd_ref[at, 0:HEAD]
        grad = qd_ref[at, HEAD : 2 * HEAD]
        scaled = q.astype(F32) * (SCALE * LOG2E)
        high = scaled.astype(BF16)
        q2_ref[:, 0:HEAD] = high
        q2_ref[:, HEAD : 2 * HEAD] = (scaled - high.astype(F32)).astype(BF16)

        def scores(i, top):
            r = rows(i, key_block)
            s = dot(kk_ref[r, :], q2_ref[...], NT)
            s_ref[r, :] = s
            return jnp.maximum(top, jnp.max(s.reshape(key_block // 8, 8, query_block), axis=0))

        top = lax.fori_loop(0, chunks, scores, jnp.full((8, query_block), -jnp.inf, F32))
        top = jnp.max(top, axis=0, keepdims=True)

        def weigh(i, total):
            r = rows(i, key_block)
            e = jnp.exp2(s_ref[r, :] - top).astype(BF16)
            e_ref[r, :] = e
            return total + dot(vt_ref[:, r], e, NN)

        total = lax.fori_loop(0, chunks, weigh, jnp.zeros((HEAD + 16, query_block), F32))
        inverse = 1.0 / total[HEAD : HEAD + 1, :]
        attended = (total[0:HEAD, :] * inverse).T.astype(BF16)
        oq_ref[at, 0:HEAD] = attended
        row_dots = jnp.sum(
            grad.astype(F32) * attended.astype(F32), axis=1, keepdims=True
        )
        dots_high = row_dots.astype(BF16).astype(F32)
        lane = lax.broadcasted_iota(jnp.int32, (query_block, HEAD), 1)
        da_ref[:, 0:HEAD] = grad
        da_ref[:, HEAD : 2 * HEAD] = jnp.where(
            lane == 0, -dots_high, jnp.where(lane == 1, dots_high - row_dots, 0.0)
        ).astype(BF16)
        inverse_column = jnp.broadcast_to(inverse, (8, query_block)).T[:, 0:1]
        grad_over = (grad.astype(F32) * inverse_column).astype(BF16)
        query_over = (q.astype(F32) * (inverse_column * SCALE)).astype(BF16)

        def back(i, total):
            r = rows(i, key_block)
            e = e_ref[r, :]
            g = (e.astype(F32) * dot(va_ref[r, :], da_ref[...], NT)).astype(BF16)
            dv = dot(e, grad_over, NN)
            dk = dot(g, query_over, NN)

            @pl.when(b == 0)
            def _():
                dv_ref[r, :] = dv
                dk_ref[r, :] = dk

            @pl.when(b > 0)
            def _():
                dv_ref[r, :] += dv
                dk_ref[r, :] += dk

            return total + dot(kt_ref[:, r], g, NN)

        total = lax.fori_loop(0, chunks, back, jnp.zeros((HEAD, query_block), F32))
        oq_ref[at, HEAD : 2 * HEAD] = (total * (inverse * SCALE)).T.astype(BF16)
        return 0

    lax.fori_loop(0, queries // query_block, block, 0)
    near_ref[:, 0:HEAD] = dk_ref[0:half, :]
    near_ref[:, HEAD : 2 * HEAD] = dv_ref[0:half, :]
    far_ref[:, 0:HEAD] = dk_ref[half:keys, :].astype(BF16)
    far_ref[:, HEAD : 2 * HEAD] = dv_ref[half:keys, :].astype(BF16)


def attention(qd, kv, kv_far, key_block=1024, query_block=1024):
    queries, half = qd.shape[0], kv.shape[0]
    keys = 2 * half
    return pl.pallas_call(
        functools.partial(attention_kernel, key_block),
        out_shape=(
            jax.ShapeDtypeStruct((queries, 2 * HEAD), BF16),
            jax.ShapeDtypeStruct((half, 2 * HEAD), F32),
            jax.ShapeDtypeStruct((half, 2 * HEAD), BF16),
        ),
        scratch_shapes=[
            pltpu.VMEM((keys, 2 * HEAD), BF16),
            pltpu.VMEM((keys, 2 * HEAD), BF16),
            pltpu.VMEM((HEAD, keys), BF16),
            pltpu.VMEM((HEAD + 16, keys), BF16),
            pltpu.VMEM((query_block, 2 * HEAD), BF16),
            pltpu.VMEM((query_block, 2 * HEAD), BF16),
            pltpu.VMEM((keys, query_block), F32),
            pltpu.VMEM((keys, query_block), BF16),
            pltpu.VMEM((keys, HEAD), F32),
            pltpu.VMEM((keys, HEAD), F32),
        ],
        compiler_params=pltpu.CompilerParams(vmem_limit_bytes=VMEM_LIMIT),
        cost_estimate=pl.CostEstimate(
            flops=12 * queries * keys * HEAD,
            bytes_accessed=12 * queries * HEAD,
            transcendentals=queries * keys,
        ),
        name="attention",
    )(qd, kv, kv_far)


def pack_kernel(q_ref, k_ref, v_ref, g_ref, out_ref):
    out_ref[0, 0, :, 0:HEAD] = q_ref[...]
    out_ref[0, 0, :, HEAD : 2 * HEAD] = g_ref[...]
    out_ref[0, 1, :, 0:HEAD] = k_ref[...]
    out_ref[0, 1, :, HEAD : 2 * HEAD] = v_ref[...]


def pack(queries, keys, values, grad_out):
    tokens = queries.shape[0]
    spec = pl.BlockSpec((tokens, HEAD), lambda h: (0, h))
    return pl.pallas_call(
        pack_kernel,
        grid=(HEADS,),
        in_specs=[spec] * 4,
        out_specs=pl.BlockSpec((1, 2, tokens, 2 * HEAD), lambda h: (h, 0, 0, 0)),
        out_shape=jax.ShapeDtypeStruct((HEADS, 2, tokens, 2 * HEAD), BF16),
        name="pack",
    )(queries, keys, values, grad_out)


def join_kernel(oq_ref, near_ref, far_ref, out_ref):
    out_ref[0, 0] = oq_ref[...]
    out_ref[0, 1] = (near_ref[...] + far_ref[...].astype(F32)).astype(BF16)


def join(oq, near, far):
    tokens = oq.shape[0] // HEADS
    spec = pl.BlockSpec((tokens, 2 * HEAD), lambda h: (h, 0))
    return pl.pallas_call(
        join_kernel,
        grid=(HEADS,),
        in_specs=[spec] * 3,
        out_specs=pl.BlockSpec((1, 2, tokens, 2 * HEAD), lambda h: (h, 0, 0, 0)),
        out_shape=jax.ShapeDtypeStruct((HEADS, 2, tokens, 2 * HEAD), BF16),
        name="join",
    )(oq, near, far)


def unpack_kernel(in_ref, o_ref, dq_ref, dk_ref, dv_ref):
    o_ref[...] = in_ref[0, 0, :, 0:HEAD]
    dq_ref[...] = in_ref[0, 0, :, HEAD : 2 * HEAD]
    dk_ref[...] = in_ref[0, 1, :, 0:HEAD]
    dv_ref[...] = in_ref[0, 1, :, HEAD : 2 * HEAD]


def unpack(packed):
    tokens = packed.shape[2]
    spec = pl.BlockSpec((tokens, HEAD), lambda h: (0, h))
    return pl.pallas_call(
        unpack_kernel,
        grid=(HEADS,),
        in_specs=[pl.BlockSpec((1, 2, tokens, 2 * HEAD), lambda h: (h, 0, 0, 0))],
        out_specs=[spec] * 4,
        out_shape=[jax.ShapeDtypeStruct((tokens, HEADS * HEAD), BF16)] * 4,
        name="unpack",
    )(packed)


def on_device(queries, keys, values, grad_out):
    members = lax.axis_size("ctx")
    same_core = [list(range(core, members, 2)) for core in range(2)]
    other_core = [(i, i ^ 1) for i in range(members)]
    swap = functools.partial(
        lax.all_to_all,
        axis_name="ctx",
        split_axis=0,
        concat_axis=0,
        tiled=True,
        axis_index_groups=same_core,
    )
    got = swap(pack(queries, keys, values, grad_out))
    tokens = queries.shape[0]
    qd = got[:, 0].reshape(HEADS * tokens, 2 * HEAD)
    kv = got[:, 1].reshape(HEADS * tokens, 2 * HEAD)
    kv_far = lax.ppermute(kv, "ctx", other_core)
    oq, near, far = attention(qd, kv, kv_far)
    far = lax.ppermute(far, "ctx", other_core)
    return tuple(unpack(swap(join(oq, near, far))))


def solution(mesh):
    spec = P(("dp", "ctx"), None)
    return jax.shard_map(
        on_device,
        mesh=mesh,
        in_specs=(spec,) * 4,
        out_specs=(spec,) * 4,
        check_vma=False,
    )
```

```python
import functools

import jax
import jax.numpy as jnp
from jax import lax
from jax.experimental import pallas as pl
from jax.experimental.pallas import tpu as pltpu
from jax.sharding import PartitionSpec as P

HEAD = 128
HEADS = 8
SCALE = HEAD**-0.5
LOG2E = 1.4426950408889634
F32 = jnp.float32
BF16 = jnp.bfloat16
NN = (((1,), (0,)), ((), ()))
NT = (((1,), (1,)), ((), ()))
VMEM_LIMIT = 60 * 2**20


def dot(a, b, dims):
    return lax.dot_general(a, b, dims, preferred_element_type=F32)


def rows(i, size):
    return pl.ds(pl.multiple_of(i * size, size), size)


def lanes(shape):
    return lax.broadcasted_iota(jnp.int32, shape, 1)


def attend_kernel(
    key_block,
    got_ref,
    far_ref,
    out_ref,
    dv_far_ref,
    grad_ref,
    query_ref,
    inverse_ref,
    weights_hbm,
    kk_ref,
    vt_ref,
    q2_ref,
    m_ref,
    total_ref,
    e_ref,
    over_ref,
    sem,
):
    blocks, _, tokens, _ = got_ref.shape
    half = blocks * tokens
    keys = 2 * half
    queries = half
    chunks = keys // key_block
    half_chunks = chunks // 2
    per_chunk = key_block // tokens

    def prepare(load, base, top):
        def step(i, top):
            pair = load(pl.ds(i * per_chunk, per_chunk)).reshape(key_block, 2 * HEAD)
            k = pair[:, 0:HEAD]
            to = rows(i + base, key_block)
            kk_ref[to, 0:HEAD] = k
            kk_ref[to, HEAD : 2 * HEAD] = k
            vt_ref[0:HEAD, to] = pair[:, HEAD : 2 * HEAD].T
            vt_ref[HEAD : HEAD + 16, to] = jnp.ones((16, key_block), BF16)
            return jnp.maximum(top, dot(ones, k * k, NT))

        return lax.fori_loop(0, half_chunks, step, top)

    ones = jnp.ones((8, HEAD), BF16)
    top = jnp.zeros((8, key_block), F32)
    top = prepare(lambda at: got_ref[at, 1], 0, top)
    top = prepare(lambda at: far_ref[at], half_chunks, top)
    top = jnp.max(top, axis=1, keepdims=True)[0:1, :]

    for i in range(blocks):
        to = slice(i * tokens, (i + 1) * tokens)
        q = got_ref[i, 0, :, 0:HEAD]
        scaled = q.astype(F32) * (SCALE * LOG2E)
        high = scaled.astype(BF16)
        q2_ref[to, 0:HEAD] = high
        q2_ref[to, HEAD : 2 * HEAD] = (scaled - high.astype(F32)).astype(BF16)
        size = dot(ones, q * q, NT)[0:1, :]
        m_ref[:, to] = jnp.sqrt(size * top) * (1.01 * SCALE * LOG2E)

    def scores(i):
        return dot(kk_ref[rows(i, key_block), :], q2_ref[...], NT)

    def weigh():
        total_ref[...] = jnp.zeros_like(total_ref)

        def step(i, _):
            r = rows(i, key_block)
            e = jnp.exp2(scores(i) - m_ref[...]).astype(BF16)
            e_ref[r, :] = e
            total_ref[...] += dot(vt_ref[:, r], e, NN)
            return 0

        lax.fori_loop(0, chunks, step, 0)

    weigh()

    @pl.when(jnp.min(total_ref[HEAD : HEAD + 1, :]) < 2.0**-80)
    def _():
        def step(i, top):
            s = scores(i).reshape(key_block // 8, 8, queries)
            return jnp.maximum(top, jnp.max(s, axis=0))

        top = lax.fori_loop(0, chunks, step, jnp.full((8, queries), -jnp.inf, F32))
        m_ref[...] = jnp.max(top, axis=0, keepdims=True)
        weigh()

    inverse = 1.0 / total_ref[HEAD : HEAD + 1, :]
    inverse_ref[...] = jnp.broadcast_to(inverse, inverse_ref.shape)
    for i in range(blocks):
        to = slice(i * tokens, (i + 1) * tokens)
        part = jnp.broadcast_to(inverse[:, to], (HEAD, tokens))
        attended = (total_ref[0:HEAD, to] * part).T.astype(BF16)
        out_ref[to, 0:HEAD] = attended
        column = part.T
        grad = got_ref[i, 0, :, HEAD : 2 * HEAD]
        grad_wide = grad.astype(F32)
        dots = jnp.sum(grad_wide * attended.astype(F32), axis=1, keepdims=True)
        dots_high = dots.astype(BF16).astype(F32)
        lane = lanes((tokens, HEAD))
        grad_ref[to, 0:HEAD] = grad
        grad_ref[to, HEAD : 2 * HEAD] = jnp.where(
            lane == 0, -dots_high, jnp.where(lane == 1, dots_high - dots, 0.0)
        ).astype(BF16)
        over_ref[to, :] = (grad_wide * column).astype(BF16)
        q = got_ref[i, 0, :, 0:HEAD].astype(F32)
        query_ref[to, :] = (q * (column * SCALE)).astype(BF16)

    def send(i):
        r = rows(i, key_block)
        return pltpu.make_async_copy(e_ref.at[r, :], weights_hbm.at[r, :], sem.at[i])

    for i in range(chunks):
        send(i).start()

    def far(i, _):
        r = rows(i + half_chunks, key_block)
        dv_far_ref[rows(i, key_block), :] = dot(e_ref[r, :], over_ref[...], NN).astype(BF16)
        return 0

    def near(i, _):
        r = rows(i, key_block)
        out_ref[r, HEAD : 2 * HEAD] = dot(e_ref[r, :], over_ref[...], NN).astype(BF16)
        return 0

    lax.fori_loop(0, half_chunks, far, 0)
    lax.fori_loop(0, half_chunks, near, 0)
    for i in range(chunks):
        send(i).wait()


def attend(got, far, key_block=1024):
    blocks, _, tokens, _ = got.shape
    half = blocks * tokens
    keys = 2 * half
    vmem = pl.BlockSpec(memory_space=pltpu.VMEM)
    return pl.pallas_call(
        functools.partial(attend_kernel, key_block),
        out_shape=(
            jax.ShapeDtypeStruct((half, 2 * HEAD), BF16),
            jax.ShapeDtypeStruct((half, HEAD), BF16),
            jax.ShapeDtypeStruct((half, 2 * HEAD), BF16),
            jax.ShapeDtypeStruct((half, HEAD), BF16),
            jax.ShapeDtypeStruct((8, half), F32),
            jax.ShapeDtypeStruct((keys, half), BF16),
        ),
        out_specs=(vmem,) * 5 + (pl.BlockSpec(memory_space=pl.ANY),),
        scratch_shapes=[
            pltpu.VMEM((keys, 2 * HEAD), BF16),
            pltpu.VMEM((HEAD + 16, keys), BF16),
            pltpu.VMEM((half, 2 * HEAD), BF16),
            pltpu.VMEM((1, half), F32),
            pltpu.VMEM((HEAD + 16, half), F32),
            pltpu.VMEM((keys, half), BF16),
            pltpu.VMEM((half, HEAD), BF16),
            pltpu.SemaphoreType.DMA((keys // key_block,)),
        ],
        compiler_params=pltpu.CompilerParams(vmem_limit_bytes=VMEM_LIMIT),
        cost_estimate=pl.CostEstimate(
            flops=6 * half * keys * HEAD,
            bytes_accessed=2 * half * keys,
            transcendentals=half * keys,
        ),
        name="attend",
    )(got, far)


def grads_kernel(
    got_ref,
    far_ref,
    grad_ref,
    query_ref,
    inverse_ref,
    e_ref,
    out_ref,
    dk_far_ref,
    kt_ref,
    va_ref,
    total_ref,
):
    i = pl.program_id(0)
    chunks = pl.num_programs(0)
    half_chunks = chunks // 2
    key_block = e_ref.shape[0]
    tokens = got_ref.shape[2]
    per_chunk = key_block // tokens

    @pl.when(i == 0)
    def _():
        total_ref[...] = jnp.zeros_like(total_ref)
        lane = lanes((key_block, HEAD))
        va_ref[:, HEAD : 2 * HEAD] = jnp.where(lane < 2, 1.0, 0.0).astype(BF16)

    def take(pair):
        pair = pair.reshape(key_block, 2 * HEAD)
        kt_ref[...] = pair[:, 0:HEAD].T
        va_ref[:, 0:HEAD] = pair[:, HEAD : 2 * HEAD]

    @pl.when(i < half_chunks)
    def _():
        take(far_ref[pl.ds(i * per_chunk, per_chunk)])

    @pl.when(i >= half_chunks)
    def _():
        take(got_ref[pl.ds((i - half_chunks) * per_chunk, per_chunk), 1])

    g = (e_ref[...].astype(F32) * dot(va_ref[...], grad_ref[...], NT)).astype(BF16)
    dk = dot(g, query_ref[...], NN).astype(BF16)
    total_ref[...] += dot(kt_ref[...], g, NN)

    @pl.when(i < half_chunks)
    def _():
        dk_far_ref[rows(i, key_block), :] = dk

    @pl.when(i >= half_chunks)
    def _():
        out_ref[rows(i - half_chunks, key_block), HEAD : 2 * HEAD] = dk

    @pl.when(i == chunks - 1)
    def _():
        scaled = total_ref[...] * (inverse_ref[0:1, :] * SCALE)
        out_ref[:, 0:HEAD] = scaled.T.astype(BF16)


def grads(got, far, grad, query, inverse, weights, key_block=1024):
    blocks, _, tokens, _ = got.shape
    half = blocks * tokens
    keys = 2 * half
    chunks = keys // key_block
    whole = pl.BlockSpec(memory_space=pltpu.VMEM)
    return pl.pallas_call(
        grads_kernel,
        grid=(chunks,),
        in_specs=[whole] * 5
        + [pl.BlockSpec((key_block, half), lambda i: ((i + chunks // 2) % chunks, 0))],
        out_specs=(whole, whole),
        out_shape=(
            jax.ShapeDtypeStruct((half, 2 * HEAD), BF16),
            jax.ShapeDtypeStruct((half, HEAD), BF16),
        ),
        scratch_shapes=[
            pltpu.VMEM((HEAD, key_block), BF16),
            pltpu.VMEM((key_block, 2 * HEAD), BF16),
            pltpu.VMEM((HEAD, half), F32),
        ],
        compiler_params=pltpu.CompilerParams(vmem_limit_bytes=VMEM_LIMIT),
        cost_estimate=pl.CostEstimate(
            flops=6 * half * keys * HEAD, bytes_accessed=2 * half * keys, transcendentals=0
        ),
        name="grads",
    )(got, far, grad, query, inverse, weights)


ANY = pl.BlockSpec(memory_space=pl.ANY)


def pack_kernel(q_ref, k_ref, v_ref, g_ref, out_ref, buffer, in_sem, out_sem):
    sources = (q_ref, g_ref, k_ref, v_ref)
    loads = [
        pltpu.make_async_copy(ref, buffer.at[i], in_sem.at[i]) for i, ref in enumerate(sources)
    ]
    for load in loads:
        load.start()
    stores = []
    for i, load in enumerate(loads):
        load.wait()
        for h in range(HEADS):
            store = pltpu.make_async_copy(
                buffer.at[i, :, h * HEAD : (h + 1) * HEAD],
                out_ref.at[h, i // 2, :, (i % 2) * HEAD : (i % 2 + 1) * HEAD],
                out_sem.at[i, h],
            )
            store.start()
            stores.append(store)
    for store in stores:
        store.wait()


def pack(queries, keys, values, grad_out):
    tokens = queries.shape[0]
    return pl.pallas_call(
        pack_kernel,
        in_specs=[ANY] * 4,
        out_specs=ANY,
        out_shape=jax.ShapeDtypeStruct((HEADS, 2, tokens, 2 * HEAD), BF16),
        scratch_shapes=[
            pltpu.VMEM((4, tokens, HEADS * HEAD), BF16),
            pltpu.SemaphoreType.DMA((4,)),
            pltpu.SemaphoreType.DMA((4, HEADS)),
        ],
        name="pack",
    )(queries, keys, values, grad_out)


def join_kernel(out_in_ref, far_ref, out_ref, near_buffer, far_buffer, sem):
    del out_in_ref
    part = out_ref.at[:, HEAD : 2 * HEAD]
    loads = (
        pltpu.make_async_copy(part, near_buffer, sem.at[0]),
        pltpu.make_async_copy(far_ref, far_buffer, sem.at[1]),
    )
    for load in loads:
        load.start()
    for load in loads:
        load.wait()
    near_buffer[...] = (near_buffer[...].astype(F32) + far_buffer[...].astype(F32)).astype(BF16)
    store = pltpu.make_async_copy(near_buffer, part, sem.at[2])
    store.start()
    store.wait()


def join(out, far):
    return pl.pallas_call(
        join_kernel,
        in_specs=[ANY] * 2,
        out_specs=ANY,
        out_shape=jax.ShapeDtypeStruct(out.shape, BF16),
        input_output_aliases={0: 0},
        scratch_shapes=[
            pltpu.VMEM(far.shape, BF16),
            pltpu.VMEM(far.shape, BF16),
            pltpu.SemaphoreType.DMA((3,)),
        ],
        name="join",
    )(out, far)


def unpack_kernel(in_ref, first_ref, second_ref, buffer, in_sem, out_sem):
    loads = [
        [
            pltpu.make_async_copy(
                in_ref.at[h, :, i * HEAD : (i + 1) * HEAD],
                buffer.at[i, :, h * HEAD : (h + 1) * HEAD],
                in_sem.at[i, h],
            )
            for h in range(HEADS)
        ]
        for i in range(2)
    ]
    for load in loads[0] + loads[1]:
        load.start()
    stores = []
    for i, ref in enumerate((first_ref, second_ref)):
        for load in loads[i]:
            load.wait()
        store = pltpu.make_async_copy(buffer.at[i], ref, out_sem.at[i])
        store.start()
        stores.append(store)
    for store in stores:
        store.wait()


def unpack(packed):
    tokens = packed.shape[1]
    whole = jax.ShapeDtypeStruct((tokens, HEADS * HEAD), BF16)
    return pl.pallas_call(
        unpack_kernel,
        in_specs=[ANY],
        out_specs=(ANY, ANY),
        out_shape=(whole, whole),
        scratch_shapes=[
            pltpu.VMEM((2, tokens, HEADS * HEAD), BF16),
            pltpu.SemaphoreType.DMA((2, HEADS)),
            pltpu.SemaphoreType.DMA((2,)),
        ],
        name="unpack",
    )(packed)


def on_device(queries, keys, values, grad_out):
    members = lax.axis_size("ctx")
    same_core = [list(range(core, members, 2)) for core in range(2)]
    other_core = [(i, i ^ 1) for i in range(members)]

    def swap(array):
        return lax.all_to_all(
            array, "ctx", 0, 0, tiled=True, axis_index_groups=same_core
        )

    def back(out, far):
        out = join(out, lax.ppermute(far, "ctx", other_core))
        return swap(out.reshape(HEADS, -1, 2 * HEAD))

    got = swap(pack(queries, keys, values, grad_out))
    far = lax.ppermute(got[:, 1], "ctx", other_core)
    first, dv_far, *rest = attend(got, far)
    first = back(first, dv_far)
    second, dk_far = grads(got, far, *rest)
    second = back(second, dk_far)
    attended, value_grads = unpack(first)
    query_grads, key_grads = unpack(second)
    return attended, query_grads, key_grads, value_grads


def solution(mesh):
    spec = P(("dp", "ctx"), None)
    return jax.shard_map(
        on_device,
        mesh=mesh,
        in_specs=(spec,) * 4,
        out_specs=(spec,) * 4,
        check_vma=False,
    )
```

```python
import functools

import jax
import jax.numpy as jnp
from jax import lax
from jax.experimental import pallas as pl
from jax.experimental.pallas import tpu as pltpu
from jax.sharding import PartitionSpec as P

HEAD = 128
HEADS = 8
SCALE = HEAD**-0.5
LOG2E = 1.4426950408889634
F32 = jnp.float32
BF16 = jnp.bfloat16
NN = (((1,), (0,)), ((), ()))
NT = (((1,), (1,)), ((), ()))
VMEM_LIMIT = 46 * 2**20
SMALL = 8 * 2**20
ANY = pl.BlockSpec(memory_space=pl.ANY)
VMEM = pl.BlockSpec(memory_space=pltpu.VMEM)


def dot(a, b, dims):
    return lax.dot_general(a, b, dims, preferred_element_type=F32)


def rows(i, size):
    return pl.ds(pl.multiple_of(i * size, size), size)


def lanes(shape):
    return lax.broadcasted_iota(jnp.int32, shape, 1)


def attention_kernel(*refs):
    chunks = refs[11].shape[0]
    for step in range(2 * chunks):
        attention_step(step, *refs)


def when(condition):
    if isinstance(condition, bool):
        return (lambda f: f()) if condition else (lambda f: None)
    return pl.when(condition)


def attention_step(
    step,
    got_ref,
    far_ref,
    out_ref,
    far_out_ref,
    kk_ref,
    vt_ref,
    kt_ref,
    va_ref,
    q2_ref,
    m_ref,
    total_ref,
    e_ref,
    grad_ref,
    grad_over_ref,
    query_over_ref,
):
    blocks, _, tokens, _ = got_ref.shape
    half = blocks * tokens
    chunks, key_block, queries = e_ref.shape
    half_chunks = chunks // 2
    per_chunk = key_block // tokens
    ones = jnp.ones((8, HEAD), BF16)

    def span(i):
        return slice(i * key_block, (i + 1) * key_block) if isinstance(i, int) else rows(i, key_block)

    def scores(i):
        return dot(kk_ref[span(i), :], q2_ref[...], NT)

    def weigh(i):
        e = jnp.exp2(scores(i) - m_ref[...]).astype(BF16)
        e_ref[i] = e
        total_ref[...] += dot(vt_ref[:, span(i)], e, NN)

    @when(step == 0)
    def _():
        def prepare(load, base, top):
            def chunk(i, top):
                pair = load(pl.ds(i * per_chunk, per_chunk)).reshape(key_block, 2 * HEAD)
                k = pair[:, 0:HEAD]
                to = rows(i + base, key_block)
                kk_ref[to, 0:HEAD] = k
                kk_ref[to, HEAD : 2 * HEAD] = k
                vt_ref[0:HEAD, to] = pair[:, HEAD : 2 * HEAD].T
                vt_ref[HEAD : HEAD + 16, to] = jnp.ones((16, key_block), BF16)
                return jnp.maximum(top, dot(ones, k * k, NT))

            return lax.fori_loop(0, half_chunks, chunk, top)

        top = jnp.zeros((8, key_block), F32)
        top = prepare(lambda at: got_ref[at, 1], 0, top)
        top = prepare(lambda at: far_ref[at], half_chunks, top)
        top = jnp.max(top, axis=1, keepdims=True)[0:1, :]
        for i in range(blocks):
            to = slice(i * tokens, (i + 1) * tokens)
            q = got_ref[i, 0, :, 0:HEAD]
            scaled = q.astype(F32) * (SCALE * LOG2E)
            high = scaled.astype(BF16)
            q2_ref[to, 0:HEAD] = high
            q2_ref[to, HEAD : 2 * HEAD] = (scaled - high.astype(F32)).astype(BF16)
            size = dot(ones, q * q, NT)[0:1, :]
            m_ref[:, to] = jnp.sqrt(size * top) * (1.01 * SCALE * LOG2E)
        total_ref[...] = jnp.zeros_like(total_ref)
        lane = lanes((key_block, HEAD))
        va_ref[:, HEAD : 2 * HEAD] = jnp.where(lane < 2, 1.0, 0.0).astype(BF16)

    @when(step < chunks)
    def _():
        weigh(step)

    @when(step == chunks)
    def _():
        @when(jnp.min(total_ref[HEAD : HEAD + 1, :]) < 2.0**-80)
        def _():
            def chunk(i, top):
                s = scores(i).reshape(key_block // 8, 8, queries)
                return jnp.maximum(top, jnp.max(s, axis=0))

            top = lax.fori_loop(0, chunks, chunk, jnp.full((8, queries), -jnp.inf, F32))
            m_ref[...] = jnp.max(top, axis=0, keepdims=True)
            total_ref[...] = jnp.zeros_like(total_ref)

            def again(i, _):
                weigh(i)
                return 0

            lax.fori_loop(0, chunks, again, 0)

        inverse = 1.0 / total_ref[HEAD : HEAD + 1, :]
        m_ref[...] = inverse
        for i in range(blocks):
            to = slice(i * tokens, (i + 1) * tokens)
            part = jnp.broadcast_to(inverse[:, to], (HEAD, tokens))
            attended = (total_ref[0:HEAD, to] * part).T.astype(BF16)
            out_ref[i, 0, :, 0:HEAD] = attended
            column = part.T
            grad = got_ref[i, 0, :, HEAD : 2 * HEAD]
            grad_wide = grad.astype(F32)
            dots = jnp.sum(grad_wide * attended.astype(F32), axis=1, keepdims=True)
            dots_high = dots.astype(BF16).astype(F32)
            lane = lanes((tokens, HEAD))
            grad_ref[to, 0:HEAD] = grad
            grad_ref[to, HEAD : 2 * HEAD] = jnp.where(
                lane == 0, -dots_high, jnp.where(lane == 1, dots_high - dots, 0.0)
            ).astype(BF16)
            grad_over_ref[to, :] = (grad_wide * column).astype(BF16)
            q = got_ref[i, 0, :, 0:HEAD].astype(F32)
            query_over_ref[to, :] = (q * (column * SCALE)).astype(BF16)
        total_ref[...] = jnp.zeros_like(total_ref)

    @when(step >= chunks)
    def _():
        i = step - chunks
        is_far = i < half_chunks
        at = pl.ds(i % half_chunks * per_chunk, per_chunk)

        def take(pair):
            pair = pair.reshape(key_block, 2 * HEAD)
            kt_ref[...] = pair[:, 0:HEAD].T
            va_ref[:, 0:HEAD] = pair[:, HEAD : 2 * HEAD]

        @when(is_far)
        def _():
            take(far_ref[at])

        @when(not is_far)
        def _():
            take(got_ref[at, 1])

        e = e_ref[(i + half_chunks) % chunks]
        dv = dot(e, grad_over_ref[...], NN).astype(BF16)
        g = (e.astype(F32) * dot(va_ref[...], grad_ref[...], NT)).astype(BF16)
        dk = dot(g, query_over_ref[...], NN).astype(BF16)
        total_ref[0:HEAD, :] += dot(kt_ref[...], g, NN)

        if is_far:
            far_out_ref[span(i), 0:HEAD] = dk
            far_out_ref[span(i), HEAD : 2 * HEAD] = dv
        else:
            to = slice((i - half_chunks) * per_chunk, (i - half_chunks + 1) * per_chunk)
            out_ref[to, 1, :, 0:HEAD] = dk.reshape(per_chunk, tokens, HEAD)
            out_ref[to, 1, :, HEAD : 2 * HEAD] = dv.reshape(per_chunk, tokens, HEAD)

    @when(step == 2 * chunks - 1)
    def _():
        for i in range(blocks):
            to = slice(i * tokens, (i + 1) * tokens)
            scaled = total_ref[0:HEAD, to] * (m_ref[:, to] * SCALE)
            out_ref[i, 0, :, HEAD : 2 * HEAD] = scaled.T.astype(BF16)


def attention(got, far, key_block=1024):
    blocks, _, tokens, _ = got.shape
    half = blocks * tokens
    keys = 2 * half
    chunks = keys // key_block
    return pl.pallas_call(
        attention_kernel,
        in_specs=[VMEM, VMEM],
        out_specs=(VMEM, VMEM),
        out_shape=(
            jax.ShapeDtypeStruct(got.shape, BF16),
            jax.ShapeDtypeStruct((half, 2 * HEAD), BF16),
        ),
        scratch_shapes=[
            pltpu.VMEM((keys, 2 * HEAD), BF16),
            pltpu.VMEM((HEAD + 16, keys), BF16),
            pltpu.VMEM((HEAD, key_block), BF16),
            pltpu.VMEM((key_block, 2 * HEAD), BF16),
            pltpu.VMEM((half, 2 * HEAD), BF16),
            pltpu.VMEM((1, half), F32),
            pltpu.VMEM((HEAD + 16, half), F32),
            pltpu.VMEM((chunks, key_block, half), BF16),
            pltpu.VMEM((half, 2 * HEAD), BF16),
            pltpu.VMEM((half, HEAD), BF16),
            pltpu.VMEM((half, HEAD), BF16),
        ],
        compiler_params=pltpu.CompilerParams(vmem_limit_bytes=VMEM_LIMIT),
        cost_estimate=pl.CostEstimate(
            flops=12 * half * keys * HEAD,
            bytes_accessed=12 * half * HEAD,
            transcendentals=half * keys,
        ),
        name="attention",
    )(got, far)


def pack_kernel(q_ref, k_ref, v_ref, g_ref, out_ref, buffer, in_sem, out_sem):
    sources = (q_ref, g_ref, k_ref, v_ref)
    loads = [
        pltpu.make_async_copy(ref, buffer.at[i], in_sem.at[i]) for i, ref in enumerate(sources)
    ]
    for load in loads:
        load.start()
    stores = []
    for i, load in enumerate(loads):
        load.wait()
        for h in range(HEADS):
            store = pltpu.make_async_copy(
                buffer.at[i, :, h * HEAD : (h + 1) * HEAD],
                out_ref.at[h, i // 2, :, (i % 2) * HEAD : (i % 2 + 1) * HEAD],
                out_sem.at[i, h],
            )
            store.start()
            stores.append(store)
    for store in stores:
        store.wait()


def pack(queries, keys, values, grad_out):
    tokens = queries.shape[0]
    return pl.pallas_call(
        pack_kernel,
        in_specs=[ANY] * 4,
        out_specs=ANY,
        out_shape=jax.ShapeDtypeStruct((HEADS, 2, tokens, 2 * HEAD), BF16),
        scratch_shapes=[
            pltpu.VMEM((4, tokens, HEADS * HEAD), BF16),
            pltpu.SemaphoreType.DMA((5,)),
            pltpu.SemaphoreType.DMA((4, HEADS)),
        ],
        name="pack",
    )(queries, keys, values, grad_out)


def join_kernel(in_ref, far_ref, out_ref):
    blocks, _, tokens, _ = in_ref.shape
    out_ref[:, 0] = in_ref[:, 0]
    for i in range(blocks):
        near = in_ref[i, 1].astype(F32)
        far = far_ref[i * tokens : (i + 1) * tokens, :].astype(F32)
        out_ref[i, 1] = (near + far).astype(BF16)


def join(out, far):
    return pl.pallas_call(
        join_kernel,
        in_specs=[VMEM] * 2,
        out_specs=VMEM,
        out_shape=jax.ShapeDtypeStruct(out.shape, BF16),
        compiler_params=pltpu.CompilerParams(vmem_limit_bytes=SMALL),
        name="join",
    )(out, far)


def unpack_kernel(in_ref, *refs):
    *outs, sem = refs
    stores = [
        pltpu.make_async_copy(
            in_ref.at[h, i // 2, :, (i % 2) * HEAD : (i % 2 + 1) * HEAD],
            ref.at[:, h * HEAD : (h + 1) * HEAD],
            sem.at[i, h],
        )
        for i, ref in enumerate(outs)
        for h in range(HEADS)
    ]
    for store in stores:
        store.start()
    for store in stores:
        store.wait()


def unpack(packed):
    tokens = packed.shape[2]
    whole = jax.ShapeDtypeStruct((tokens, HEADS * HEAD), BF16)
    return pl.pallas_call(
        unpack_kernel,
        in_specs=[VMEM],
        out_specs=(ANY,) * 4,
        out_shape=(whole,) * 4,
        scratch_shapes=[pltpu.SemaphoreType.DMA((4, HEADS))],
        compiler_params=pltpu.CompilerParams(vmem_limit_bytes=SMALL),
        name="unpack",
    )(packed)


def on_device(queries, keys, values, grad_out):
    members = lax.axis_size("ctx")
    same_core = [list(range(core, members, 2)) for core in range(2)]
    other_core = [(i, i ^ 1) for i in range(members)]

    def swap(array):
        return lax.all_to_all(
            array, "ctx", 0, 0, tiled=True, axis_index_groups=same_core
        )

    def other(array):
        return lax.ppermute(array, "ctx", other_core)

    got = swap(pack(queries, keys, values, grad_out))
    out, far = attention(got, other(got[:, 1]))
    return tuple(unpack(swap(join(out, other(far)))))


def solution(mesh):
    spec = P(("dp", "ctx"), None)
    return jax.shard_map(
        on_device,
        mesh=mesh,
        in_specs=(spec,) * 4,
        out_specs=(spec,) * 4,
        check_vma=False,
    )
```

```python
import functools

import jax
import jax.numpy as jnp
from jax import lax
from jax.experimental import pallas as pl
from jax.experimental.pallas import tpu as pltpu
from jax.sharding import PartitionSpec as P

HEAD = 128
HEADS = 8
SCALE = HEAD**-0.5
LOG2E = 1.4426950408889634
F32 = jnp.float32
BF16 = jnp.bfloat16
NN = (((1,), (0,)), ((), ()))
NT = (((1,), (1,)), ((), ()))
VMEM_LIMIT = 46 * 2**20
SMALL = 8 * 2**20
ANY = pl.BlockSpec(memory_space=pl.ANY)
VMEM = pl.BlockSpec(memory_space=pltpu.VMEM)
ROW = 4
HOPS = ((0, 0), (1, 2), (1, 1), (1, 3), (1, 0), (0, 2), (0, 1), (0, 3))


def chip_at(chip, hop, sign=1):
    x, z = chip // ROW, chip % ROW
    return (x + hop[0]) % 2 * ROW + (z + sign * hop[1] + ROW) % ROW


def dot(a, b, dims):
    return lax.dot_general(a, b, dims, preferred_element_type=F32)


def rows(i, size):
    return pl.ds(pl.multiple_of(i * size, size), size)


def lanes(shape):
    return lax.broadcasted_iota(jnp.int32, shape, 1)


def attention_kernel(*refs):
    got, refs = refs[:HEADS], refs[HEADS:]
    chunks = refs[10].shape[0]
    for step in range(2 * chunks):
        attention_step(step, got, *refs)


def when(condition):
    if isinstance(condition, bool):
        return (lambda f: f()) if condition else (lambda f: None)
    return pl.when(condition)


def attention_step(
    step,
    got,
    far_ref,
    out_ref,
    far_out_ref,
    kk_ref,
    vt_ref,
    kt_ref,
    va_ref,
    q2_ref,
    m_ref,
    total_ref,
    e_ref,
    grad_ref,
    grad_over_ref,
    query_over_ref,
):
    blocks = len(got)
    tokens = got[0].shape[1]
    half = blocks * tokens
    chunks, key_block, queries = e_ref.shape
    half_chunks = chunks // 2
    per_chunk = key_block // tokens
    ones = jnp.ones((8, HEAD), BF16)

    def span(i):
        return slice(i * key_block, (i + 1) * key_block) if isinstance(i, int) else rows(i, key_block)

    def scores(i):
        return dot(kk_ref[span(i), :], q2_ref[...], NT)

    def weigh(i):
        e = jnp.exp2(scores(i) - m_ref[...]).astype(BF16)
        e_ref[i] = e
        total_ref[...] += dot(vt_ref[:, span(i)], e, NN)

    @when(step == 0)
    def _():
        top = jnp.zeros((8, tokens), F32)
        for i in range(2 * blocks):
            pair = got[i][1] if i < blocks else far_ref[i - blocks]
            k = pair[:, 0:HEAD]
            to = slice(i * tokens, (i + 1) * tokens)
            kk_ref[to, 0:HEAD] = k
            kk_ref[to, HEAD : 2 * HEAD] = k
            vt_ref[0:HEAD, to] = pair[:, HEAD : 2 * HEAD].T
            vt_ref[HEAD : HEAD + 16, to] = jnp.ones((16, tokens), BF16)
            top = jnp.maximum(top, dot(ones, k * k, NT))
        top = jnp.max(top, axis=1, keepdims=True)[0:1, :]
        for i in range(blocks):
            to = slice(i * tokens, (i + 1) * tokens)
            q = got[i][0, :, 0:HEAD]
            scaled = q.astype(F32) * (SCALE * LOG2E)
            high = scaled.astype(BF16)
            q2_ref[to, 0:HEAD] = high
            q2_ref[to, HEAD : 2 * HEAD] = (scaled - high.astype(F32)).astype(BF16)
            size = dot(ones, q * q, NT)[0:1, :]
            m_ref[:, to] = jnp.sqrt(size * top) * (1.01 * SCALE * LOG2E)
        total_ref[...] = jnp.zeros_like(total_ref)
        lane = lanes((key_block, HEAD))
        va_ref[:, HEAD : 2 * HEAD] = jnp.where(lane < 2, 1.0, 0.0).astype(BF16)

    @when(step < chunks)
    def _():
        weigh(step)

    @when(step == chunks)
    def _():
        @when(jnp.min(total_ref[HEAD : HEAD + 1, :]) < 2.0**-80)
        def _():
            def chunk(i, top):
                s = scores(i).reshape(key_block // 8, 8, queries)
                return jnp.maximum(top, jnp.max(s, axis=0))

            top = lax.fori_loop(0, chunks, chunk, jnp.full((8, queries), -jnp.inf, F32))
            m_ref[...] = jnp.max(top, axis=0, keepdims=True)
            total_ref[...] = jnp.zeros_like(total_ref)

            def again(i, _):
                weigh(i)
                return 0

            lax.fori_loop(0, chunks, again, 0)

        inverse = 1.0 / total_ref[HEAD : HEAD + 1, :]
        m_ref[...] = inverse
        for i in range(blocks):
            to = slice(i * tokens, (i + 1) * tokens)
            part = jnp.broadcast_to(inverse[:, to], (HEAD, tokens))
            attended = (total_ref[0:HEAD, to] * part).T.astype(BF16)
            out_ref[i, 0, :, 0:HEAD] = attended
            column = part.T
            grad = got[i][0, :, HEAD : 2 * HEAD]
            grad_wide = grad.astype(F32)
            dots = jnp.sum(grad_wide * attended.astype(F32), axis=1, keepdims=True)
            dots_high = dots.astype(BF16).astype(F32)
            lane = lanes((tokens, HEAD))
            grad_ref[to, 0:HEAD] = grad
            grad_ref[to, HEAD : 2 * HEAD] = jnp.where(
                lane == 0, -dots_high, jnp.where(lane == 1, dots_high - dots, 0.0)
            ).astype(BF16)
            grad_over_ref[to, :] = (grad_wide * column).astype(BF16)
            q = got[i][0, :, 0:HEAD].astype(F32)
            query_over_ref[to, :] = (q * (column * SCALE)).astype(BF16)
        total_ref[...] = jnp.zeros_like(total_ref)

    @when(step >= chunks)
    def _():
        i = step - chunks
        is_far = i < half_chunks
        for j in range(per_chunk):
            block = i % half_chunks * per_chunk + j
            pair = far_ref[block] if is_far else got[block][1]
            to = slice(j * tokens, (j + 1) * tokens)
            kt_ref[:, to] = pair[:, 0:HEAD].T
            va_ref[to, 0:HEAD] = pair[:, HEAD : 2 * HEAD]

        e = e_ref[(i + half_chunks) % chunks]
        dv = dot(e, grad_over_ref[...], NN).astype(BF16)
        g = (e.astype(F32) * dot(va_ref[...], grad_ref[...], NT)).astype(BF16)
        dk = dot(g, query_over_ref[...], NN).astype(BF16)
        total_ref[0:HEAD, :] += dot(kt_ref[...], g, NN)

        if is_far:
            far_out_ref[span(i), 0:HEAD] = dk
            far_out_ref[span(i), HEAD : 2 * HEAD] = dv
        else:
            to = slice((i - half_chunks) * per_chunk, (i - half_chunks + 1) * per_chunk)
            out_ref[to, 1, :, 0:HEAD] = dk.reshape(per_chunk, tokens, HEAD)
            out_ref[to, 1, :, HEAD : 2 * HEAD] = dv.reshape(per_chunk, tokens, HEAD)

    @when(step == 2 * chunks - 1)
    def _():
        for i in range(blocks):
            to = slice(i * tokens, (i + 1) * tokens)
            scaled = total_ref[0:HEAD, to] * (m_ref[:, to] * SCALE)
            out_ref[i, 0, :, HEAD : 2 * HEAD] = scaled.T.astype(BF16)


def attention(got, far, key_block=1024):
    blocks, tokens = len(got), got[0].shape[1]
    half = blocks * tokens
    keys = 2 * half
    chunks = keys // key_block
    return pl.pallas_call(
        attention_kernel,
        in_specs=[VMEM] * (blocks + 1),
        out_specs=(VMEM, VMEM),
        out_shape=(
            jax.ShapeDtypeStruct((blocks, 2, tokens, 2 * HEAD), BF16),
            jax.ShapeDtypeStruct((half, 2 * HEAD), BF16),
        ),
        scratch_shapes=[
            pltpu.VMEM((keys, 2 * HEAD), BF16),
            pltpu.VMEM((HEAD + 16, keys), BF16),
            pltpu.VMEM((HEAD, key_block), BF16),
            pltpu.VMEM((key_block, 2 * HEAD), BF16),
            pltpu.VMEM((half, 2 * HEAD), BF16),
            pltpu.VMEM((1, half), F32),
            pltpu.VMEM((HEAD + 16, half), F32),
            pltpu.VMEM((chunks, key_block, half), BF16),
            pltpu.VMEM((half, 2 * HEAD), BF16),
            pltpu.VMEM((half, HEAD), BF16),
            pltpu.VMEM((half, HEAD), BF16),
        ],
        compiler_params=pltpu.CompilerParams(vmem_limit_bytes=VMEM_LIMIT),
        cost_estimate=pl.CostEstimate(
            flops=12 * half * keys * HEAD,
            bytes_accessed=12 * half * HEAD,
            transcendentals=half * keys,
        ),
        name="attention",
    )(*got, far)


def pack_kernel(q_ref, k_ref, v_ref, g_ref, *refs):
    outs, (buffer, in_sem, out_sem) = refs[:HEADS], refs[HEADS:]
    chip = lax.axis_index("ctx") // 2
    sources = (q_ref, g_ref, k_ref, v_ref)
    loads = [
        pltpu.make_async_copy(ref, buffer.at[i], in_sem.at[i]) for i, ref in enumerate(sources)
    ]
    for load in loads:
        load.start()
    stores = []
    for i, load in enumerate(loads):
        load.wait()
        for j, hop in enumerate(HOPS):
            head = pl.multiple_of(chip_at(chip, hop) * HEAD, HEAD)
            store = pltpu.make_async_copy(
                buffer.at[i, :, pl.ds(head, HEAD)],
                outs[j].at[i // 2, :, (i % 2) * HEAD : (i % 2 + 1) * HEAD],
                out_sem.at[i, j],
            )
            store.start()
            stores.append(store)
    for store in stores:
        store.wait()


def pack(queries, keys, values, grad_out):
    tokens = queries.shape[0]
    return pl.pallas_call(
        pack_kernel,
        in_specs=[ANY] * 4,
        out_specs=(ANY,) * HEADS,
        out_shape=(jax.ShapeDtypeStruct((2, tokens, 2 * HEAD), BF16),) * HEADS,
        scratch_shapes=[
            pltpu.VMEM((4, tokens, HEADS * HEAD), BF16),
            pltpu.SemaphoreType.DMA((4,)),
            pltpu.SemaphoreType.DMA((4, HEADS)),
        ],
        name="pack",
    )(queries, keys, values, grad_out)


def pairs_kernel(*refs):
    *blocks, out_ref = refs
    for i, ref in enumerate(blocks):
        out_ref[i] = ref[1]


def pairs(blocks):
    _, tokens, features = blocks[0].shape
    return pl.pallas_call(
        pairs_kernel,
        in_specs=[VMEM] * len(blocks),
        out_specs=VMEM,
        out_shape=jax.ShapeDtypeStruct((len(blocks), tokens, features), BF16),
        compiler_params=pltpu.CompilerParams(vmem_limit_bytes=SMALL),
        name="pairs",
    )(*blocks)


def join_kernel(in_ref, far_ref, *outs):
    tokens = in_ref.shape[2]
    for i, out_ref in enumerate(outs):
        out_ref[0] = in_ref[i, 0]
        near = in_ref[i, 1].astype(F32)
        far = far_ref[i * tokens : (i + 1) * tokens, :].astype(F32)
        out_ref[1] = (near + far).astype(BF16)


def join(out, far):
    blocks = out.shape[0]
    return pl.pallas_call(
        join_kernel,
        in_specs=[VMEM] * 2,
        out_specs=(VMEM,) * blocks,
        out_shape=(jax.ShapeDtypeStruct(out.shape[1:], BF16),) * blocks,
        compiler_params=pltpu.CompilerParams(vmem_limit_bytes=SMALL),
        name="join",
    )(out, far)


def unpack_kernel(*refs):
    blocks, outs, sem = refs[:HEADS], refs[HEADS:-1], refs[-1]
    chip = lax.axis_index("ctx") // 2
    stores = []
    for j, hop in enumerate(HOPS):
        head = pl.multiple_of(chip_at(chip, hop) * HEAD, HEAD)
        for i, ref in enumerate(outs):
            store = pltpu.make_async_copy(
                blocks[j].at[i // 2, :, (i % 2) * HEAD : (i % 2 + 1) * HEAD],
                ref.at[:, pl.ds(head, HEAD)],
                sem.at[i, j],
            )
            store.start()
            stores.append(store)
    for store in stores:
        store.wait()


def unpack(blocks):
    tokens = blocks[0].shape[1]
    whole = jax.ShapeDtypeStruct((tokens, HEADS * HEAD), BF16)
    return pl.pallas_call(
        unpack_kernel,
        in_specs=[VMEM] * HEADS,
        out_specs=(ANY,) * 4,
        out_shape=(whole,) * 4,
        scratch_shapes=[pltpu.SemaphoreType.DMA((4, HEADS))],
        compiler_params=pltpu.CompilerParams(vmem_limit_bytes=SMALL),
        name="unpack",
    )(*blocks)


def on_device(queries, keys, values, grad_out):
    members = lax.axis_size("ctx")
    other_core = [(i, i ^ 1) for i in range(members)]

    def other(array):
        return lax.ppermute(array, "ctx", other_core)

    def travel(blocks, sign):
        moved = [blocks[0]]
        for block, hop in zip(blocks[1:], HOPS[1:]):
            to = [(i, chip_at(i // 2, hop, sign) * 2 + i % 2) for i in range(members)]
            moved.append(lax.ppermute(block, "ctx", to))
        return moved

    got = travel(pack(queries, keys, values, grad_out), 1)
    out, far = attention(got, other(pairs(got)))
    attended, query_grads, key_grads, value_grads = unpack(travel(join(out, other(far)), -1))
    return attended, query_grads, key_grads, value_grads


def solution(mesh):
    spec = P(("dp", "ctx"), None)
    return jax.shard_map(
        on_device,
        mesh=mesh,
        in_specs=(spec,) * 4,
        out_specs=(spec,) * 4,
        check_vma=False,
    )
```

```python
import functools

import jax
import jax.numpy as jnp
from jax import lax
from jax.experimental import pallas as pl
from jax.experimental.pallas import tpu as pltpu
from jax.sharding import PartitionSpec as P

HEAD = 128
HEADS = 8
SCALE = HEAD**-0.5
LOG2E = 1.4426950408889634
F32 = jnp.float32
BF16 = jnp.bfloat16
NN = (((1,), (0,)), ((), ()))
NT = (((1,), (1,)), ((), ()))
VMEM_LIMIT = 46 * 2**20
SMALL = 8 * 2**20
ANY = pl.BlockSpec(memory_space=pl.ANY)
VMEM = pl.BlockSpec(memory_space=pltpu.VMEM)
ROW = 4
EARLY = 4
LATE = 5
HOPS = ((0, 0), (1, 2), (1, 1), (1, 3), (1, 0), (0, 2), (0, 1), (0, 3))


def chip_at(chip, hop, sign=1):
    x, z = chip // ROW, chip % ROW
    return (x + hop[0]) % 2 * ROW + (z + sign * hop[1] + ROW) % ROW


def dot(a, b, dims):
    return lax.dot_general(a, b, dims, preferred_element_type=F32)


def rows(i, size):
    return pl.ds(pl.multiple_of(i * size, size), size)


def lanes(shape):
    return lax.broadcasted_iota(jnp.int32, shape, 1)


def attention_kernel(*refs):
    got, far, refs = refs[:HEADS], refs[HEADS : HEADS + 2], refs[HEADS + 2 :]
    far = [part.at[i] for part in far for i in range(part.shape[0])]
    chunks = refs[9].shape[0]
    for step in range(2 * chunks):
        attention_step(step, got, far, *refs)


def when(condition):
    if isinstance(condition, bool):
        return (lambda f: f()) if condition else (lambda f: None)
    return pl.when(condition)


def attention_step(
    step,
    got,
    far,
    out_ref,
    far_out_ref,
    kk_ref,
    vt_ref,
    kt_ref,
    va_ref,
    q2_ref,
    m_ref,
    total_ref,
    e_ref,
    grad_ref,
    grad_over_ref,
    query_over_ref,
):
    blocks = len(got)
    tokens = got[0].shape[1]
    half = blocks * tokens
    chunks, key_block, queries = e_ref.shape
    half_chunks = chunks // 2
    per_chunk = key_block // tokens
    ones = jnp.ones((8, HEAD), BF16)

    def span(i):
        return slice(i * key_block, (i + 1) * key_block) if isinstance(i, int) else rows(i, key_block)

    def scores(i):
        return dot(kk_ref[span(i), :], q2_ref[...], NT)

    def weigh(i):
        e = jnp.exp2(scores(i) - m_ref[...]).astype(BF16)
        e_ref[i] = e
        total_ref[...] += dot(vt_ref[:, span(i)], e, NN)

    @when(step == 0)
    def _():
        top = jnp.zeros((8, tokens), F32)
        for i in range(2 * blocks):
            pair = got[i][1] if i < blocks else far[i - blocks][...]
            k = pair[:, 0:HEAD]
            to = slice(i * tokens, (i + 1) * tokens)
            kk_ref[to, 0:HEAD] = k
            kk_ref[to, HEAD : 2 * HEAD] = k
            vt_ref[0:HEAD, to] = pair[:, HEAD : 2 * HEAD].T
            vt_ref[HEAD : HEAD + 16, to] = jnp.ones((16, tokens), BF16)
            top = jnp.maximum(top, dot(ones, k * k, NT))
        top = jnp.max(top, axis=1, keepdims=True)[0:1, :]
        for i in range(blocks):
            to = slice(i * tokens, (i + 1) * tokens)
            q = got[i][0, :, 0:HEAD]
            scaled = q.astype(F32) * (SCALE * LOG2E)
            high = scaled.astype(BF16)
            q2_ref[to, 0:HEAD] = high
            q2_ref[to, HEAD : 2 * HEAD] = (scaled - high.astype(F32)).astype(BF16)
            size = dot(ones, q * q, NT)[0:1, :]
            m_ref[:, to] = jnp.sqrt(size * top) * (1.01 * SCALE * LOG2E)
        total_ref[...] = jnp.zeros_like(total_ref)
        lane = lanes((key_block, HEAD))
        va_ref[:, HEAD : 2 * HEAD] = jnp.where(lane < 2, 1.0, 0.0).astype(BF16)

    @when(step < chunks)
    def _():
        weigh(step)

    @when(step == chunks)
    def _():
        @when(jnp.min(total_ref[HEAD : HEAD + 1, :]) < 2.0**-80)
        def _():
            def chunk(i, top):
                s = scores(i).reshape(key_block // 8, 8, queries)
                return jnp.maximum(top, jnp.max(s, axis=0))

            top = lax.fori_loop(0, chunks, chunk, jnp.full((8, queries), -jnp.inf, F32))
            m_ref[...] = jnp.max(top, axis=0, keepdims=True)
            total_ref[...] = jnp.zeros_like(total_ref)

            def again(i, _):
                weigh(i)
                return 0

            lax.fori_loop(0, chunks, again, 0)

        inverse = 1.0 / total_ref[HEAD : HEAD + 1, :]
        m_ref[...] = inverse
        for i in range(blocks):
            to = slice(i * tokens, (i + 1) * tokens)
            part = jnp.broadcast_to(inverse[:, to], (HEAD, tokens))
            attended = (total_ref[0:HEAD, to] * part).T.astype(BF16)
            out_ref[i, 0, :, 0:HEAD] = attended
            column = part.T
            grad = got[i][0, :, HEAD : 2 * HEAD]
            grad_wide = grad.astype(F32)
            dots = jnp.sum(grad_wide * attended.astype(F32), axis=1, keepdims=True)
            dots_high = dots.astype(BF16).astype(F32)
            lane = lanes((tokens, HEAD))
            grad_ref[to, 0:HEAD] = grad
            grad_ref[to, HEAD : 2 * HEAD] = jnp.where(
                lane == 0, -dots_high, jnp.where(lane == 1, dots_high - dots, 0.0)
            ).astype(BF16)
            grad_over_ref[to, :] = (grad_wide * column).astype(BF16)
            q = got[i][0, :, 0:HEAD].astype(F32)
            query_over_ref[to, :] = (q * (column * SCALE)).astype(BF16)
        total_ref[...] = jnp.zeros_like(total_ref)

    @when(step >= chunks)
    def _():
        i = step - chunks
        is_far = i < half_chunks
        for j in range(per_chunk):
            block = i % half_chunks * per_chunk + j
            pair = far[block][...] if is_far else got[block][1]
            to = slice(j * tokens, (j + 1) * tokens)
            kt_ref[:, to] = pair[:, 0:HEAD].T
            va_ref[to, 0:HEAD] = pair[:, HEAD : 2 * HEAD]

        e = e_ref[(i + half_chunks) % chunks]
        dv = dot(e, grad_over_ref[...], NN).astype(BF16)
        g = (e.astype(F32) * dot(va_ref[...], grad_ref[...], NT)).astype(BF16)
        dk = dot(g, query_over_ref[...], NN).astype(BF16)
        total_ref[0:HEAD, :] += dot(kt_ref[...], g, NN)

        if is_far:
            far_out_ref[span(i), 0:HEAD] = dk
            far_out_ref[span(i), HEAD : 2 * HEAD] = dv
        else:
            to = slice((i - half_chunks) * per_chunk, (i - half_chunks + 1) * per_chunk)
            out_ref[to, 1, :, 0:HEAD] = dk.reshape(per_chunk, tokens, HEAD)
            out_ref[to, 1, :, HEAD : 2 * HEAD] = dv.reshape(per_chunk, tokens, HEAD)

    @when(step == 2 * chunks - 1)
    def _():
        for i in range(blocks):
            to = slice(i * tokens, (i + 1) * tokens)
            scaled = total_ref[0:HEAD, to] * (m_ref[:, to] * SCALE)
            out_ref[i, 0, :, HEAD : 2 * HEAD] = scaled.T.astype(BF16)


def attention(got, far, key_block=1024):
    blocks, tokens = len(got), got[0].shape[1]
    half = blocks * tokens
    keys = 2 * half
    chunks = keys // key_block
    return pl.pallas_call(
        attention_kernel,
        in_specs=[VMEM] * (blocks + 2),
        out_specs=(VMEM, VMEM),
        out_shape=(
            jax.ShapeDtypeStruct((blocks, 2, tokens, 2 * HEAD), BF16),
            jax.ShapeDtypeStruct((half, 2 * HEAD), BF16),
        ),
        scratch_shapes=[
            pltpu.VMEM((keys, 2 * HEAD), BF16),
            pltpu.VMEM((HEAD + 16, keys), BF16),
            pltpu.VMEM((HEAD, key_block), BF16),
            pltpu.VMEM((key_block, 2 * HEAD), BF16),
            pltpu.VMEM((half, 2 * HEAD), BF16),
            pltpu.VMEM((1, half), F32),
            pltpu.VMEM((HEAD + 16, half), F32),
            pltpu.VMEM((chunks, key_block, half), BF16),
            pltpu.VMEM((half, 2 * HEAD), BF16),
            pltpu.VMEM((half, HEAD), BF16),
            pltpu.VMEM((half, HEAD), BF16),
        ],
        compiler_params=pltpu.CompilerParams(vmem_limit_bytes=VMEM_LIMIT),
        cost_estimate=pl.CostEstimate(
            flops=12 * half * keys * HEAD,
            bytes_accessed=12 * half * HEAD,
            transcendentals=half * keys,
        ),
        name="attention",
    )(*got, *far)


def pack_kernel(q_ref, k_ref, v_ref, g_ref, *refs):
    outs, (buffer, in_sem, out_sem) = refs[:HEADS], refs[HEADS:]
    chip = lax.axis_index("ctx") // 2
    sources = (q_ref, g_ref, k_ref, v_ref)
    loads = [
        pltpu.make_async_copy(ref, buffer.at[i], in_sem.at[i]) for i, ref in enumerate(sources)
    ]
    for load in loads:
        load.start()
    stores = []
    for i, load in enumerate(loads):
        load.wait()
        for j, hop in enumerate(HOPS):
            head = pl.multiple_of(chip_at(chip, hop) * HEAD, HEAD)
            store = pltpu.make_async_copy(
                buffer.at[i, :, pl.ds(head, HEAD)],
                outs[j].at[i // 2, :, (i % 2) * HEAD : (i % 2 + 1) * HEAD],
                out_sem.at[i, j],
            )
            store.start()
            stores.append(store)
    for store in stores:
        store.wait()


def pack(queries, keys, values, grad_out):
    tokens = queries.shape[0]
    return pl.pallas_call(
        pack_kernel,
        in_specs=[ANY] * 4,
        out_specs=(ANY,) * HEADS,
        out_shape=(jax.ShapeDtypeStruct((2, tokens, 2 * HEAD), BF16),) * HEADS,
        scratch_shapes=[
            pltpu.VMEM((4, tokens, HEADS * HEAD), BF16),
            pltpu.SemaphoreType.DMA((4,)),
            pltpu.SemaphoreType.DMA((4, HEADS)),
        ],
        name="pack",
    )(queries, keys, values, grad_out)


def pairs_kernel(*refs):
    *blocks, out_ref = refs
    for i, ref in enumerate(blocks):
        out_ref[i] = ref[1]


def pairs(blocks):
    _, tokens, features = blocks[0].shape
    return pl.pallas_call(
        pairs_kernel,
        in_specs=[VMEM] * len(blocks),
        out_specs=VMEM,
        out_shape=jax.ShapeDtypeStruct((len(blocks), tokens, features), BF16),
        compiler_params=pltpu.CompilerParams(vmem_limit_bytes=SMALL),
        name="pairs",
    )(*blocks)


def join_kernel(in_ref, far_ref, *outs):
    tokens = in_ref.shape[2]
    for i, out_ref in enumerate(outs):
        out_ref[0] = in_ref[i, 0]
        near = in_ref[i, 1].astype(F32)
        far = far_ref[i * tokens : (i + 1) * tokens, :].astype(F32)
        out_ref[1] = (near + far).astype(BF16)


def join(out, far):
    blocks = out.shape[0]
    return pl.pallas_call(
        join_kernel,
        in_specs=[VMEM] * 2,
        out_specs=(VMEM,) * blocks,
        out_shape=(jax.ShapeDtypeStruct(out.shape[1:], BF16),) * blocks,
        compiler_params=pltpu.CompilerParams(vmem_limit_bytes=SMALL),
        name="join",
    )(out, far)


def unpack_kernel(first, count, *refs):
    blocks, outs, sem = refs[:count], refs[-5:-1], refs[-1]
    chip = lax.axis_index("ctx") // 2
    stores = []
    for j, hop in enumerate(HOPS[first : first + count]):
        head = pl.multiple_of(chip_at(chip, hop) * HEAD, HEAD)
        for i, ref in enumerate(outs):
            store = pltpu.make_async_copy(
                blocks[j].at[i // 2, :, (i % 2) * HEAD : (i % 2 + 1) * HEAD],
                ref.at[:, pl.ds(head, HEAD)],
                sem.at[i, j],
            )
            store.start()
            stores.append(store)
    for store in stores:
        store.wait()


def unpack(blocks, first, outs=()):
    tokens, count = blocks[0].shape[1], len(blocks)
    whole = jax.ShapeDtypeStruct((tokens, HEADS * HEAD), BF16)
    return pl.pallas_call(
        functools.partial(unpack_kernel, first, count),
        in_specs=[VMEM] * count + [ANY] * len(outs),
        out_specs=(ANY,) * 4,
        out_shape=(whole,) * 4,
        input_output_aliases={count + i: i for i in range(len(outs))},
        scratch_shapes=[pltpu.SemaphoreType.DMA((4, count))],
        compiler_params=pltpu.CompilerParams(vmem_limit_bytes=SMALL),
        name="unpack",
    )(*blocks, *outs)


def on_device(queries, keys, values, grad_out):
    members = lax.axis_size("ctx")
    other_core = [(i, i ^ 1) for i in range(members)]

    def other(array):
        return lax.ppermute(array, "ctx", other_core)

    def travel(blocks, sign):
        moved = [blocks[0]]
        for block, hop in zip(blocks[1:], HOPS[1:]):
            to = [(i, chip_at(i // 2, hop, sign) * 2 + i % 2) for i in range(members)]
            moved.append(lax.ppermute(block, "ctx", to))
        return moved

    got = travel(pack(queries, keys, values, grad_out), 1)
    far = [other(pairs(got[:EARLY])), other(pairs(got[EARLY:]))]
    out, far = attention(got, far)
    back = travel(join(out, other(far)), -1)
    outs = unpack(back[:LATE], 0)
    return tuple(unpack(back[LATE:], LATE, outs))


def solution(mesh):
    spec = P(("dp", "ctx"), None)
    return jax.shard_map(
        on_device,
        mesh=mesh,
        in_specs=(spec,) * 4,
        out_specs=(spec,) * 4,
        check_vma=False,
    )
```

```python
import functools

import jax
import jax.numpy as jnp
from jax import lax
from jax.experimental import pallas as pl
from jax.experimental.pallas import tpu as pltpu
from jax.sharding import PartitionSpec as P

HEAD = 128
HEADS = 8
SCALE = HEAD**-0.5
LOG2E = 1.4426950408889634
F32 = jnp.float32
BF16 = jnp.bfloat16
NN = (((1,), (0,)), ((), ()))
NT = (((1,), (1,)), ((), ()))
VMEM_LIMIT = 46 * 2**20
SMALL = 8 * 2**20
ANY = pl.BlockSpec(memory_space=pl.ANY)
VMEM = pl.BlockSpec(memory_space=pltpu.VMEM)
ROW = 4
EARLY = 4
LATE = 5
HOPS = ((0, 0), (1, 2), (1, 1), (1, 3), (1, 0), (0, 2), (0, 1), (0, 3))


def chip_at(chip, hop, sign=1):
    x, z = chip // ROW, chip % ROW
    return (x + hop[0]) % 2 * ROW + (z + sign * hop[1] + ROW) % ROW


def dot(a, b, dims):
    return lax.dot_general(a, b, dims, preferred_element_type=F32)


def rows(i, size):
    return pl.ds(pl.multiple_of(i * size, size), size)


def lanes(shape):
    return lax.broadcasted_iota(jnp.int32, shape, 1)


def attention_kernel(*refs):
    got, far, refs = refs[:HEADS], refs[HEADS : HEADS + 2], refs[HEADS + 2 :]
    far = [part.at[i] for part in far for i in range(part.shape[0])]
    out, far_outs, refs = refs[0], refs[1:3], refs[3:]
    chunks = refs[7].shape[0]
    for step in range(2 * chunks):
        attention_step(step, got, far, out, far_outs, *refs)


def when(condition):
    if isinstance(condition, bool):
        return (lambda f: f()) if condition else (lambda f: None)
    return pl.when(condition)


def attention_step(
    step,
    got,
    far,
    out_ref,
    far_outs,
    kk_ref,
    vt_ref,
    kt_ref,
    va_ref,
    q2_ref,
    m_ref,
    total_ref,
    e_ref,
    grad_ref,
    grad_over_ref,
    query_over_ref,
):
    blocks = len(got)
    tokens = got[0].shape[1]
    half = blocks * tokens
    chunks, key_block, queries = e_ref.shape
    half_chunks = chunks // 2
    per_chunk = key_block // tokens
    ones = jnp.ones((8, HEAD), BF16)

    def span(i):
        return slice(i * key_block, (i + 1) * key_block) if isinstance(i, int) else rows(i, key_block)

    def scores(i):
        return dot(kk_ref[span(i), :], q2_ref[...], NT)

    def weigh(i):
        e = jnp.exp2(scores(i) - m_ref[...]).astype(BF16)
        e_ref[i] = e
        total_ref[...] += dot(vt_ref[:, span(i)], e, NN)

    @when(step == 0)
    def _():
        top = jnp.zeros((8, tokens), F32)
        for i in range(2 * blocks):
            pair = got[i][1] if i < blocks else far[i - blocks][...]
            k = pair[:, 0:HEAD]
            to = slice(i * tokens, (i + 1) * tokens)
            kk_ref[to, 0:HEAD] = k
            kk_ref[to, HEAD : 2 * HEAD] = k
            vt_ref[0:HEAD, to] = pair[:, HEAD : 2 * HEAD].T
            vt_ref[HEAD : HEAD + 16, to] = jnp.ones((16, tokens), BF16)
            top = jnp.maximum(top, dot(ones, k * k, NT))
        top = jnp.max(top, axis=1, keepdims=True)[0:1, :]
        for i in range(blocks):
            to = slice(i * tokens, (i + 1) * tokens)
            q = got[i][0, :, 0:HEAD]
            scaled = q.astype(F32) * (SCALE * LOG2E)
            high = scaled.astype(BF16)
            q2_ref[to, 0:HEAD] = high
            q2_ref[to, HEAD : 2 * HEAD] = (scaled - high.astype(F32)).astype(BF16)
            size = dot(ones, q * q, NT)[0:1, :]
            m_ref[:, to] = jnp.sqrt(size * top) * (1.01 * SCALE * LOG2E)
        total_ref[...] = jnp.zeros_like(total_ref)
        lane = lanes((key_block, HEAD))
        va_ref[:, HEAD : 2 * HEAD] = jnp.where(lane < 2, 1.0, 0.0).astype(BF16)

    @when(step < chunks)
    def _():
        weigh(step)

    @when(step == chunks)
    def _():
        @when(jnp.min(total_ref[HEAD : HEAD + 1, :]) < 2.0**-80)
        def _():
            def chunk(i, top):
                s = scores(i).reshape(key_block // 8, 8, queries)
                return jnp.maximum(top, jnp.max(s, axis=0))

            top = lax.fori_loop(0, chunks, chunk, jnp.full((8, queries), -jnp.inf, F32))
            m_ref[...] = jnp.max(top, axis=0, keepdims=True)
            total_ref[...] = jnp.zeros_like(total_ref)

            def again(i, _):
                weigh(i)
                return 0

            lax.fori_loop(0, chunks, again, 0)

        inverse = 1.0 / total_ref[HEAD : HEAD + 1, :]
        m_ref[...] = inverse
        for i in range(blocks):
            to = slice(i * tokens, (i + 1) * tokens)
            part = jnp.broadcast_to(inverse[:, to], (HEAD, tokens))
            attended = (total_ref[0:HEAD, to] * part).T.astype(BF16)
            out_ref[i, 0, :, 0:HEAD] = attended
            column = part.T
            grad = got[i][0, :, HEAD : 2 * HEAD]
            grad_wide = grad.astype(F32)
            dots = jnp.sum(grad_wide * attended.astype(F32), axis=1, keepdims=True)
            dots_high = dots.astype(BF16).astype(F32)
            lane = lanes((tokens, HEAD))
            grad_ref[to, 0:HEAD] = grad
            grad_ref[to, HEAD : 2 * HEAD] = jnp.where(
                lane == 0, -dots_high, jnp.where(lane == 1, dots_high - dots, 0.0)
            ).astype(BF16)
            grad_over_ref[to, :] = (grad_wide * column).astype(BF16)
            q = got[i][0, :, 0:HEAD].astype(F32)
            query_over_ref[to, :] = (q * (column * SCALE)).astype(BF16)
        total_ref[...] = jnp.zeros_like(total_ref)

    @when(step >= chunks)
    def _():
        i = step - chunks
        is_far = i < half_chunks
        for j in range(per_chunk):
            block = i % half_chunks * per_chunk + j
            pair = far[block][...] if is_far else got[block][1]
            to = slice(j * tokens, (j + 1) * tokens)
            kt_ref[:, to] = pair[:, 0:HEAD].T
            va_ref[to, 0:HEAD] = pair[:, HEAD : 2 * HEAD]

        e = e_ref[(i + half_chunks) % chunks]
        dv = dot(e, grad_over_ref[...], NN).astype(BF16)
        g = (e.astype(F32) * dot(va_ref[...], grad_ref[...], NT)).astype(BF16)
        dk = dot(g, query_over_ref[...], NN).astype(BF16)
        total_ref[0:HEAD, :] += dot(kt_ref[...], g, NN)

        if is_far:
            far_outs[i][:, 0:HEAD] = dk
            far_outs[i][:, HEAD : 2 * HEAD] = dv
        else:
            to = slice((i - half_chunks) * per_chunk, (i - half_chunks + 1) * per_chunk)
            out_ref[to, 1, :, 0:HEAD] = dk.reshape(per_chunk, tokens, HEAD)
            out_ref[to, 1, :, HEAD : 2 * HEAD] = dv.reshape(per_chunk, tokens, HEAD)

    @when(step == 2 * chunks - 1)
    def _():
        for i in range(blocks):
            to = slice(i * tokens, (i + 1) * tokens)
            scaled = total_ref[0:HEAD, to] * (m_ref[:, to] * SCALE)
            out_ref[i, 0, :, HEAD : 2 * HEAD] = scaled.T.astype(BF16)


def attention(got, far, key_block=1024):
    blocks, tokens = len(got), got[0].shape[1]
    half = blocks * tokens
    keys = 2 * half
    chunks = keys // key_block
    return pl.pallas_call(
        attention_kernel,
        in_specs=[VMEM] * (blocks + 2),
        out_specs=(VMEM,) * 3,
        out_shape=(
            jax.ShapeDtypeStruct((blocks, 2, tokens, 2 * HEAD), BF16),
            *[jax.ShapeDtypeStruct((key_block, 2 * HEAD), BF16)] * (half // key_block),
        ),
        scratch_shapes=[
            pltpu.VMEM((keys, 2 * HEAD), BF16),
            pltpu.VMEM((HEAD + 16, keys), BF16),
            pltpu.VMEM((HEAD, key_block), BF16),
            pltpu.VMEM((key_block, 2 * HEAD), BF16),
            pltpu.VMEM((half, 2 * HEAD), BF16),
            pltpu.VMEM((1, half), F32),
            pltpu.VMEM((HEAD + 16, half), F32),
            pltpu.VMEM((chunks, key_block, half), BF16),
            pltpu.VMEM((half, 2 * HEAD), BF16),
            pltpu.VMEM((half, HEAD), BF16),
            pltpu.VMEM((half, HEAD), BF16),
        ],
        compiler_params=pltpu.CompilerParams(vmem_limit_bytes=VMEM_LIMIT),
        cost_estimate=pl.CostEstimate(
            flops=12 * half * keys * HEAD,
            bytes_accessed=12 * half * HEAD,
            transcendentals=half * keys,
        ),
        name="attention",
    )(*got, *far)


def pack_kernel(q_ref, k_ref, v_ref, g_ref, *refs):
    outs, (buffer, in_sem, out_sem) = refs[:HEADS], refs[HEADS:]
    chip = lax.axis_index("ctx") // 2
    sources = (q_ref, g_ref, k_ref, v_ref)
    loads = [
        pltpu.make_async_copy(ref, buffer.at[i], in_sem.at[i]) for i, ref in enumerate(sources)
    ]
    for load in loads:
        load.start()
    stores = []
    for i, load in enumerate(loads):
        load.wait()
        for j, hop in enumerate(HOPS):
            head = pl.multiple_of(chip_at(chip, hop) * HEAD, HEAD)
            store = pltpu.make_async_copy(
                buffer.at[i, :, pl.ds(head, HEAD)],
                outs[j].at[i // 2, :, (i % 2) * HEAD : (i % 2 + 1) * HEAD],
                out_sem.at[i, j],
            )
            store.start()
            stores.append(store)
    for store in stores:
        store.wait()


def pack(queries, keys, values, grad_out):
    tokens = queries.shape[0]
    return pl.pallas_call(
        pack_kernel,
        in_specs=[ANY] * 4,
        out_specs=(ANY,) * HEADS,
        out_shape=(jax.ShapeDtypeStruct((2, tokens, 2 * HEAD), BF16),) * HEADS,
        scratch_shapes=[
            pltpu.VMEM((4, tokens, HEADS * HEAD), BF16),
            pltpu.SemaphoreType.DMA((4,)),
            pltpu.SemaphoreType.DMA((4, HEADS)),
        ],
        name="pack",
    )(queries, keys, values, grad_out)


def pairs_kernel(*refs):
    *blocks, out_ref = refs
    for i, ref in enumerate(blocks):
        out_ref[i] = ref[1]


def pairs(blocks):
    _, tokens, features = blocks[0].shape
    return pl.pallas_call(
        pairs_kernel,
        in_specs=[VMEM] * len(blocks),
        out_specs=VMEM,
        out_shape=jax.ShapeDtypeStruct((len(blocks), tokens, features), BF16),
        compiler_params=pltpu.CompilerParams(vmem_limit_bytes=SMALL),
        name="pairs",
    )(*blocks)


def join_kernel(first, in_ref, far_ref, *outs):
    tokens = in_ref.shape[2]
    for i, out_ref in enumerate(outs):
        out_ref[0] = in_ref[first + i, 0]
        near = in_ref[first + i, 1].astype(F32)
        far = far_ref[i * tokens : (i + 1) * tokens, :].astype(F32)
        out_ref[1] = (near + far).astype(BF16)


def join(out, far, first):
    blocks = far.shape[0] // out.shape[2]
    return pl.pallas_call(
        functools.partial(join_kernel, first),
        in_specs=[VMEM] * 2,
        out_specs=(VMEM,) * blocks,
        out_shape=(jax.ShapeDtypeStruct(out.shape[1:], BF16),) * blocks,
        compiler_params=pltpu.CompilerParams(vmem_limit_bytes=SMALL),
        name="join",
    )(out, far)


def unpack_kernel(first, count, *refs):
    blocks, outs, sem = refs[:count], refs[-5:-1], refs[-1]
    chip = lax.axis_index("ctx") // 2
    stores = []
    for j, hop in enumerate(HOPS[first : first + count]):
        head = pl.multiple_of(chip_at(chip, hop) * HEAD, HEAD)
        for i, ref in enumerate(outs):
            store = pltpu.make_async_copy(
                blocks[j].at[i // 2, :, (i % 2) * HEAD : (i % 2 + 1) * HEAD],
                ref.at[:, pl.ds(head, HEAD)],
                sem.at[i, j],
            )
            store.start()
            stores.append(store)
    for store in stores:
        store.wait()


def unpack(blocks, first, outs=()):
    tokens, count = blocks[0].shape[1], len(blocks)
    whole = jax.ShapeDtypeStruct((tokens, HEADS * HEAD), BF16)
    return pl.pallas_call(
        functools.partial(unpack_kernel, first, count),
        in_specs=[VMEM] * count + [ANY] * len(outs),
        out_specs=(ANY,) * 4,
        out_shape=(whole,) * 4,
        input_output_aliases={count + i: i for i in range(len(outs))},
        scratch_shapes=[pltpu.SemaphoreType.DMA((4, count))],
        compiler_params=pltpu.CompilerParams(vmem_limit_bytes=SMALL),
        name="unpack",
    )(*blocks, *outs)


def on_device(queries, keys, values, grad_out):
    members = lax.axis_size("ctx")
    other_core = [(i, i ^ 1) for i in range(members)]

    def other(array):
        return lax.ppermute(array, "ctx", other_core)

    def travel(blocks, sign):
        moved = [blocks[0]]
        for block, hop in zip(blocks[1:], HOPS[1:]):
            to = [(i, chip_at(i // 2, hop, sign) * 2 + i % 2) for i in range(members)]
            moved.append(lax.ppermute(block, "ctx", to))
        return moved

    got = travel(pack(queries, keys, values, grad_out), 1)
    far = [other(pairs(got[:EARLY])), other(pairs(got[EARLY:]))]
    out, *far = attention(got, far)
    joined = [join(out, other(part), i * HEADS // len(far)) for i, part in enumerate(far)]
    back = travel([*joined[0], *joined[1]], -1)
    outs = unpack(back[:LATE], 0)
    return tuple(unpack(back[LATE:], LATE, outs))


def solution(mesh):
    spec = P(("dp", "ctx"), None)
    return jax.shard_map(
        on_device,
        mesh=mesh,
        in_specs=(spec,) * 4,
        out_specs=(spec,) * 4,
        check_vma=False,
    )
```
